32 devices in a mesh: grp: 2 (over y), gx: 4 (over z), gy: 2 (over x), hour: 2 (over core).
Axes of the slice: x: 2, y: 2, z: 4, core: 2. Of those that a mesh axis runs over, the one named last changes fastest.
Arguments:
- control: float32 [32, 512, 1024], P(('grp', 'hour'), 'gx', 'gy'), parts along dimension 0, may hold values from -6 to 6
- background_scale: bfloat16 [32, 512, 1024], P(('grp', 'hour'), 'gx', 'gy'), parts along dimension 0, may hold values from 0.29882812 to 3
- rate_x: float32 [32, 512], P(('grp', 'hour'), 'gx'), parts along dimension 0, as said below
- rate_y: float32 [32, 1024], P(('grp', 'hour')), parts along dimension 0, as said below
- obs_owner: int32 [4096], P(('grp', 'gx', 'gy')), parts along dimension 0, may hold values from 0 to 7, as said below
- stencil: int32 [4096, 16], P(('grp', 'gx', 'gy')), parts along dimension 0, may hold values from 0 to 65535, as said below
- obs_weights: float32 [4096, 256], P(('grp', 'gx', 'gy'), 'hour'), parts along dimension 0, may hold values from -0.375 to 0.375
- innovation: float32 [4096], P(('grp', 'gx', 'gy')), parts along dimension 0, may hold values from -6 to 6
- obs_sigma: float32 [4096], P(('grp', 'gx', 'gy')), parts along dimension 0, may hold values from 0.3 to 3
Outputs:
- increment: float32 [32, 512, 1024], P(('grp', 'hour'), 'gx', 'gy'), parts along dimension 0
- departure: float32 [4096], P(('grp', 'gx', 'gy')), parts along dimension 0
The draws below stay inside these ranges and needn't reach their ends.
There are 2 independent parts, one for each index of `grp`. The reference program is written for one: setup_inputs(seed, part) draws one part's arguments, and reference() takes and returns one part's arrays. A program takes and returns all parts, laid end to end along the dimension named above; each array names one. Nothing has to cross between parts.
Inputs may be any that keep to these rules, and one draw needn't show every extreme that they name: `obs_owner`: each value is an owner index over gx+gy in mesh order. At most 64 of the observations of one device go to one owner, and in every draw one owner receives exactly 64 from every device. `stencil`: the 16 cells of an observation form a 4 by 4 block of its owner's tile of 128 by 512 cells. `rate_x`: Positive. `rate_y`: Positive.
All inputs are finite; a program needn't handle non-finite values.
Results may differ from the reference program's by a relative error of at most 0.0003.
Values sent between devices are 32-bit elements; how exact they have to be, the bound alone decides.
A program may use at most 128 MiB of HBM per device.

```python
import math
import jax
import jax.numpy as jnp
from jax import lax

LEV = 16
S = 16
CX = 128
CY = 512
OBS_DEV = 256
NX = 512
NY = 1024
OBS = 2048
N_GX = 4
N_GY = 2


def log_uniform(key, shape, low, high):
    return jnp.exp(jax.random.uniform(key, shape, jnp.float32, jnp.log(low), jnp.log(high)))


def decay_field(key, length, block_width, fast_percent):
    subkeys = jax.random.split(key, 7)
    chooser = jax.random.randint(subkeys[0], (LEV,), 0, 100) < fast_percent
    fast_rates = log_uniform(subkeys[1], (LEV,), 1.0 / 50.0, 1.0 / 30.0)
    slow_rates = log_uniform(subkeys[2], (LEV,), 0.25, 0.7) / length
    reference_attenuation_speeds = jnp.where(chooser, fast_rates, slow_rates)
    tile_scaling_factor = jnp.repeat(log_uniform(subkeys[3], (LEV, length // block_width), 0.5, 2.0), block_width, axis=1)
    ground_texture_length = jax.random.uniform(subkeys[4], (LEV, length), jnp.float32, 0.5, 1.5)
    sensor_locations = jax.random.randint(subkeys[5], (LEV, 2), 0, length)
    stratum_thickness = jax.random.uniform(subkeys[6], (LEV, 2), jnp.float32, 0.22, 0.45)
    sensor_coordinates = jnp.arange(length, dtype=jnp.int32)
    measurement_groups = jnp.sum(jnp.where(sensor_coordinates[None, :, None] == sensor_locations[:, None, :], stratum_thickness[:, None, :], 0.0), axis=2)
    return reference_attenuation_speeds[:, None] * tile_scaling_factor * ground_texture_length + measurement_groups


def draw_rate_x(key, part):
    key = jax.random.fold_in(key, 3)
    fast_percent = 50
    return decay_field(key, NX, CX, fast_percent)


def draw_rate_y(key, part):
    key = jax.random.fold_in(key, 4)
    fast_percent = 50
    return decay_field(key, NY, CY, fast_percent)


def draw_obs_owner(key, part):
    key = jax.random.fold_in(key, 5)
    owner_count = N_GX * N_GY
    capacity = 2 * OBS_DEV // owner_count
    hot_key, rest_key = jax.random.split(key)
    hottest = jax.random.randint(hot_key, (), 0, owner_count)

    def one_source(source_key):
        pool_key, order_key = jax.random.split(source_key)
        chosen = jax.random.permutation(pool_key, (owner_count - 1) * capacity)[:OBS_DEV - capacity] // capacity
        chosen = (chosen + (chosen >= hottest).astype(jnp.int32)).astype(jnp.int32)
        assigned = jnp.concatenate([jnp.zeros((capacity,), jnp.int32) + hottest, chosen])
        return jax.random.permutation(order_key, assigned)
    sources = jax.vmap(one_source)(jax.random.split(rest_key, owner_count))
    return sources.reshape(-1).astype(jnp.int32)


def draw_stencil(key, part):
    key = jax.random.fold_in(key, 7)
    corner_key, side_key = jax.random.split(key)
    corner_x = jax.random.randint(corner_key, (OBS,), 0, CX - 3)
    corner_y = jax.random.randint(side_key, (OBS,), 0, CY - 3)
    within = jnp.arange(OBS, dtype=jnp.int32) % OBS_DEV
    corner_x = jnp.where(within == 0, 0, jnp.where(within == 1, CX - 4, corner_x))
    corner_y = jnp.where(within == 0, 0, jnp.where(within == 1, CY - 4, corner_y))
    offsets = jnp.arange(S, dtype=jnp.int32)
    cells = (corner_x[:, None] + offsets[None, :] // 4) * CY + corner_y[:, None] + offsets[None, :] % 4
    return cells.astype(jnp.int32)


def block_levels(rng, shape, cuts, smallest, largest):
    level = 1.0
    for dim, shards_of in cuts:
        draws = jax.random.uniform(jax.random.fold_in(jax.random.fold_in(rng, 6), dim), (shards_of,), jnp.float32, smallest / len(cuts), largest / len(cuts))
        level = level * jnp.repeat(jnp.exp(draws), shape[dim] // shards_of).reshape((-1,) + (1,) * (len(shape) - 1 - dim))
    return level


def scatter_about(stream_key, dims, scale, bound, pieces=(), kind=jnp.bfloat16):
    values = scale * jax.random.normal(stream_key, dims, jnp.float32)
    if pieces:
        values = values * block_levels(stream_key, dims, pieces, -0.22, 0.18)
    return jnp.clip(values, -bound, bound).astype(kind)


def setup_inputs(seed: int = 0, part: int = 0) -> dict:
    keys = jax.random.split(jax.random.key(seed), 10)
    own_keys = jax.random.split(jax.random.fold_in(keys[9], part), 10)
    control = scatter_about(own_keys[0], (LEV, NX, NY), 1.0, 6.0, ((0, 2), (1, 4), (2, 2)), jnp.float32)
    background_scale = jnp.clip(jnp.exp(math.log(3.0) - 2.306499 * jax.random.uniform(own_keys[1], (LEV, NX, NY), jnp.float32) ** block_levels(own_keys[1], (LEV, NX, NY), ((0, 2), (1, 4), (2, 2)), -0.2, 0.2)), 0.29882812, 3.0).astype(jnp.bfloat16)
    rate_x = draw_rate_x(jax.random.fold_in(jax.random.fold_in(keys[9], part), 71), part)
    rate_y = draw_rate_y(jax.random.fold_in(jax.random.fold_in(keys[9], part), 71), part)
    obs_owner = draw_obs_owner(jax.random.fold_in(jax.random.fold_in(keys[9], part), 71), part)
    stencil = draw_stencil(jax.random.fold_in(jax.random.fold_in(keys[9], part), 71), part)
    obs_weights = scatter_about(own_keys[6], (OBS, LEV * S), (LEV * S) ** -0.5, 0.375, ((0, 8), (1, 2)), jnp.float32)
    innovation = scatter_about(own_keys[7], (OBS,), 1.0, 6.0, ((0, 8),), jnp.float32)
    obs_sigma = jnp.clip(jnp.exp(math.log(3.0) - 2.3025851 * jax.random.uniform(own_keys[8], (OBS,), jnp.float32) ** block_levels(own_keys[8], (OBS,), ((0, 8),), -0.2, 0.2)), 0.3, 3.0)
    return dict(control=control, background_scale=background_scale, rate_x=rate_x, rate_y=rate_y, obs_owner=obs_owner, stencil=stencil, obs_weights=obs_weights, innovation=innovation, obs_sigma=obs_sigma)


EXACT = lax.Precision.HIGHEST

def recursive_pass(field, rates):
    decays = jnp.exp(-rates)
    gain_forward = jnp.sqrt(-jnp.expm1(-2.0 * rates))
    gain_backward = -jnp.expm1(-rates)
    columns = jnp.moveaxis(field, 1, 0)

    def forward_step(carried, inputs):
        column_value, factor, weight = inputs
        carried = factor[:, None] * carried + weight[:, None] * column_value
        return (carried, carried)

    def backward_step(carried, inputs):
        column_value, factor, weight = inputs
        carried = factor[:, None] * carried + weight[:, None] * column_value
        return (carried, carried)
    initial = jnp.zeros_like(columns[0])
    _, smooth = lax.scan(forward_step, initial, (columns, decays.T, gain_forward.T))
    _, result = lax.scan(backward_step, initial, (smooth, decays.T, gain_backward.T), reverse=True)
    return jnp.moveaxis(result, 0, 1)

def reference(control, background_scale, rate_x, rate_y, obs_owner, stencil, obs_weights, innovation, obs_sigma):
    along_x = recursive_pass(control, rate_x)
    filtered = jnp.swapaxes(recursive_pass(jnp.swapaxes(along_x, 1, 2), rate_y), 1, 2)
    increment = filtered * background_scale.astype(jnp.float32)
    tile_x = obs_owner // N_GY
    tile_y = obs_owner % N_GY
    cell_x = (tile_x[:, None] * CX + stencil // CY).astype(jnp.int32)
    cell_y = (tile_y[:, None] * CY + stencil % CY).astype(jnp.int32)
    sampled = increment[:, cell_x, cell_y]
    shaped = obs_weights.reshape(OBS, LEV, S)
    modelled = jnp.einsum('kls,lks->k', shaped, sampled, precision=EXACT)
    departure = (modelled - innovation) / obs_sigma
    return (increment, departure)
```

```python
import functools

import jax
import jax.numpy as jnp
from jax import lax
from jax.experimental import pallas as pl
from jax.experimental.pallas import tpu as pltpu
from jax.sharding import PartitionSpec as P

EXACT = lax.Precision.HIGHEST
MESH = pl.DeviceIdType.MESH
LANES = 128


def coefficients(rate):
    a = jnp.exp(-rate)
    series = jnp.ones_like(rate)
    small = jnp.minimum(rate, 0.5)
    for n in range(9, 1, -1):
        series = 1.0 - series * small * (1.0 / n)
    c = jnp.where(rate < 0.5, small * series, 1.0 - a)
    b = jnp.sqrt(c * (1.0 + a))
    return a, b, c


def pick(row, index):
    return jnp.take_along_axis(row, index, axis=1, mode="promise_in_bounds")


def combine(edges, carries, count, width):
    zero = tuple(jnp.zeros(edges.shape[2:], jnp.float32) for _ in range(width))

    def ahead(e, state):
        for t in range(width):
            carries[e, t] = state[t]
        factor = edges[e, 2 * width]
        return tuple(factor * state[t] + edges[e, t] for t in range(width))

    def behind(k, state):
        e = count - 1 - k
        for t in range(width):
            carries[e, width + t] = state[t]
        factor = edges[e, 2 * width]
        cross = edges[e, 2 * width + 1]
        return tuple(
            factor * state[t] + (edges[e, width + t] + cross * carries[e, t])
            for t in range(width)
        )

    if count <= 8:
        state = zero
        for e in range(count):
            state = ahead(e, state)
        state = zero
        for k in range(count):
            state = behind(k, state)
    else:
        lax.fori_loop(0, count, ahead, zero)
        lax.fori_loop(0, count, behind, zero)


def kernel(
    dims,
    control,
    scale,
    rate_x_h,
    rate_y_h,
    owner_h,
    stencil_h,
    weights_h,
    innovation_h,
    sigma_h,
    out,
    departure,
    field,
    scale_v,
    zx,
    zy,
    v1x,
    v2x,
    v1y,
    v2y,
    edges_x,
    edges_y,
    carry_x,
    carry_y,
    send_obs,
    recv_obs,
    codes_v,
    codes_s,
    acc,
    send_ret,
    recv_ret,
    rate_x,
    rate_y,
    owner,
    stencil,
    weights,
    innovation,
    sigma,
    small_sem,
    in_sem,
    out_sem,
    scale_sem,
    code_sem,
    xs,
    xr,
    ys,
    yr,
    os_,
    or_,
    rs,
    rr,
):
    nx, ny, nh, cap = dims
    owners = nx * ny
    levels, cx, cy = control.shape
    tiles = cy // LANES
    obs = owner.shape[1]
    mx, my, mh = lax.axis_index("gx"), lax.axis_index("gy"), lax.axis_index("hour")
    me = mx * ny + my
    world = owners * nh
    rank = me * nh + mh

    barrier = pltpu.get_barrier_semaphore()

    def greet(j, _):
        other = lax.rem(rank + j, world)
        pl.semaphore_signal(
            barrier,
            inc=1,
            device_id={
                "gx": other // (ny * nh),
                "gy": lax.rem(other // nh, ny),
                "hour": lax.rem(other, nh),
            },
            device_id_type=MESH,
        )
        return 0

    def load(t, l):
        return pltpu.make_async_copy(
            control.at[l, :, pl.ds(t * LANES, LANES)],
            field.at[t, pl.ds(l * cx, cx), :],
            in_sem.at[t, l],
        )

    small = [
        pltpu.make_async_copy(source, place, small_sem.at[n])
        for n, (source, place) in enumerate(
            (
                (rate_x_h, rate_x),
                (owner_h, owner),
                (stencil_h, stencil),
                (weights_h, weights),
                (rate_y_h, rate_y),
                (innovation_h, innovation),
                (sigma_h, sigma),
            )
        )
    ]
    small[0].start()
    for t in range(tiles):
        for l in range(levels):
            load(t, l).start()
    for copy in small[1:]:
        copy.start()
    scale_copy = pltpu.make_async_copy(scale, scale_v, scale_sem)
    scale_copy.start()
    lax.fori_loop(1, world, greet, 0)

    lane = lax.broadcasted_iota(jnp.int32, (levels, LANES), 1)
    ones = jnp.ones((levels, LANES), jnp.float32)
    zeros = jnp.zeros((levels, LANES), jnp.float32)

    small[0].wait()
    ax, bx, cxg = coefficients(rate_x[...])
    for t in range(tiles):
        for l in range(levels):
            load(t, l).wait()

    def x_forward(i, state):
        at = lane * 0 + i
        a, b = pick(ax, at), pick(bx, at)
        row = pl.ds(pl.multiple_of(i * levels, levels), levels)
        new = []
        for t in range(tiles):
            s = a * state[t] + b * field[t, pl.ds(i, levels, stride=cx), :]
            zx[t, row, :] = s
            new.append(s)
        lead = a * state[tiles]
        v1x[row, :] = lead
        return tuple(new) + (lead,)

    state = lax.fori_loop(0, cx, x_forward, (zeros,) * tiles + (ones,), unroll=8)
    for t in range(tiles):
        edges_x[mx, t] = state[t]
    edges_x[mx, 2 * tiles] = state[tiles]

    def x_backward(k, state):
        i = cx - 1 - k
        at = lane * 0 + i
        a, c = pick(ax, at), pick(cxg, at)
        row = pl.ds(pl.multiple_of(i * levels, levels), levels)
        new = []
        for t in range(tiles):
            s = a * state[t] + c * zx[t, row, :]
            zx[t, row, :] = s
            new.append(s)
        cross = a * state[tiles] + c * v1x[row, :]
        v1x[row, :] = cross
        trail = a * state[tiles + 1]
        v2x[row, :] = trail
        return tuple(new) + (cross, trail)

    state = lax.fori_loop(0, cx, x_backward, (zeros,) * (tiles + 1) + (ones,), unroll=8)
    for t in range(tiles):
        edges_x[mx, tiles + t] = state[t]
    edges_x[mx, 2 * tiles + 1] = state[tiles]

    pl.semaphore_wait(barrier, world - 1)

    def x_copy(j, place):
        return pltpu.make_async_remote_copy(
            src_ref=edges_x.at[place],
            dst_ref=edges_x.at[place],
            send_sem=xs.at[j],
            recv_sem=xr.at[j],
            device_id={"gx": lax.rem(mx + j, nx)},
            device_id_type=MESH,
        )

    def x_start(j, _):
        x_copy(j, mx).start()
        return 0

    lax.fori_loop(1, nx, x_start, 0)

    for copy in small[1:]:
        copy.wait()
    own = owner[...]
    own_col = jnp.transpose(jnp.broadcast_to(own.astype(jnp.float32), (8, obs)))[:, :1]
    earlier = lax.broadcasted_iota(jnp.int32, (obs, obs), 0) < lax.broadcasted_iota(
        jnp.int32, (obs, obs), 1
    )
    same = earlier & (own_col == own.astype(jnp.float32))
    place = jnp.sum(jnp.where(same, 1.0, 0.0), axis=0, keepdims=True).astype(jnp.int32)
    cells = stencil[...]
    points = cells.shape[0]
    corner = jnp.min(cells, axis=0, keepdims=True)
    j_row = lax.broadcasted_iota(jnp.int32, (points, obs), 0)
    wanted = corner + (j_row // 4) * cy + lax.rem(j_row, 4)
    order = jnp.zeros((points, obs), jnp.int32)
    for s in range(1, points):
        order = jnp.where(cells[s : s + 1, :] == wanted, s, order)
    order = jnp.concatenate([order + points * l for l in range(levels)], axis=0)
    order = jnp.transpose(order.astype(jnp.float32)).astype(jnp.int32)
    sorted_weights = pick(weights[...], order)
    target = own * cap + place
    slots = owners * cap
    chosen = jnp.where(
        lax.broadcasted_iota(jnp.int32, (slots, obs), 0) == target, 1.0, 0.0
    )
    packed = jnp.dot(
        chosen, sorted_weights, precision=EXACT, preferred_element_type=jnp.float32
    )
    send_obs[:, :cap, :] = packed.reshape(owners, cap, LANES)
    of_owner = jnp.where(
        lax.broadcasted_iota(jnp.int32, (owners, obs), 0) == own, 1.0, 0.0
    )
    of_place = jnp.where(
        lax.broadcasted_iota(jnp.int32, (LANES, obs), 0) == place, 1.0, 0.0
    )
    codes = lax.dot_general(
        of_owner * corner.astype(jnp.float32),
        of_place,
        (((1,), (1,)), ((), ())),
        precision=EXACT,
        preferred_element_type=jnp.float32,
    )
    send_obs[:, cap:, :] = jnp.broadcast_to(codes[:, None, :], (owners, 8, LANES))
    recv_obs[me] = send_obs[me]

    def obs_copy(j, there, here):
        return pltpu.make_async_remote_copy(
            src_ref=send_obs.at[there],
            dst_ref=recv_obs.at[here],
            send_sem=os_.at[j],
            recv_sem=or_.at[j],
            device_id={"gx": there // ny, "gy": lax.rem(there, ny)},
            device_id_type=MESH,
        )

    def obs_start(j, _):
        obs_copy(j, lax.rem(me + j, owners), me).start()
        return 0

    lax.fori_loop(1, owners, obs_start, 0)

    def x_wait(j, _):
        x_copy(j, lax.rem(mx + nx - j, nx)).wait_recv()
        return 0

    lax.fori_loop(1, nx, x_wait, 0)
    combine(edges_x, carry_x, nx, tiles)
    front = [carry_x[mx, t] for t in range(tiles)]
    back = [carry_x[mx, tiles + t] for t in range(tiles)]

    def x_finish(i, _):
        row = pl.ds(pl.multiple_of(i * levels, levels), levels)
        lead, trail = v1x[row, :], v2x[row, :]
        for t in range(tiles):
            zx[t, row, :] = zx[t, row, :] + (lead * front[t] + trail * back[t])
        return 0

    lax.fori_loop(0, cx, x_finish, 0, unroll=8)

    for t in range(tiles):
        for l in range(levels):
            zy[t, pl.ds(l, LANES, stride=levels), :] = jnp.transpose(
                zx[t, pl.ds(l, cx, stride=levels), :]
            )

    gains = [
        coefficients(rate_y[:, pl.ds(pl.multiple_of(my * cy + t * LANES, LANES), LANES)])
        for t in range(tiles)
    ]

    def y_forward(j, state):
        at = lane * 0 + j
        row = pl.ds(pl.multiple_of(j * levels, levels), levels)
        new, leads = [], []
        for t in range(tiles):
            a, b = pick(gains[t][0], at), pick(gains[t][1], at)
            s = a * state[t] + b * zy[t, row, :]
            zy[t, row, :] = s
            new.append(s)
            lead = a * state[tiles + t]
            v1y[t, row, :] = lead
            leads.append(lead)
        return tuple(new + leads)

    state = lax.fori_loop(
        0, LANES, y_forward, (zeros,) * tiles + (ones,) * tiles, unroll=4
    )
    for t in range(tiles):
        edges_y[my * tiles + t, 0] = state[t]
        edges_y[my * tiles + t, 2] = state[tiles + t]

    def y_backward(k, state):
        j = LANES - 1 - k
        at = lane * 0 + j
        row = pl.ds(pl.multiple_of(j * levels, levels), levels)
        new, crosses, trails = [], [], []
        for t in range(tiles):
            a, c = pick(gains[t][0], at), pick(gains[t][2], at)
            s = a * state[t] + c * zy[t, row, :]
            zy[t, row, :] = s
            new.append(s)
            cross = a * state[tiles + t] + c * v1y[t, row, :]
            v1y[t, row, :] = cross
            crosses.append(cross)
            trail = a * state[2 * tiles + t]
            v2y[t, row, :] = trail
            trails.append(trail)
        return tuple(new + crosses + trails)

    state = lax.fori_loop(
        0, LANES, y_backward, (zeros,) * (2 * tiles) + (ones,) * tiles, unroll=4
    )
    for t in range(tiles):
        edges_y[my * tiles + t, 1] = state[t]
        edges_y[my * tiles + t, 3] = state[tiles + t]

    def y_copy(j, there):
        part = edges_y.at[pl.ds(there * tiles, tiles)]
        return pltpu.make_async_remote_copy(
            src_ref=part,
            dst_ref=part,
            send_sem=ys.at[j],
            recv_sem=yr.at[j],
            device_id={"gy": lax.rem(my + j, ny)},
            device_id_type=MESH,
        )

    for j in range(1, ny):
        y_copy(j, my).start()

    def obs_wait(j, _):
        obs_copy(j, lax.rem(me + j, owners), lax.rem(me + owners - j, owners)).wait_recv()
        return 0

    lax.fori_loop(1, owners, obs_wait, 0)
    codes_v[...] = recv_obs[:, cap, :].astype(jnp.int32)
    code_copy = pltpu.make_async_copy(codes_v, codes_s, code_sem)
    code_copy.start()
    send_ret[...] = jnp.zeros(send_ret.shape, jnp.float32)
    scale_copy.wait()

    for j in range(1, ny):
        y_copy(j, lax.rem(my + ny - j, ny)).wait_recv()
    combine(edges_y, carry_y, ny * tiles, 1)

    for t in range(tiles):
        front_y = carry_y[my * tiles + t, 0]
        back_y = carry_y[my * tiles + t, 1]

        def y_finish(j, _, t=t, front_y=front_y, back_y=back_y):
            row = pl.ds(pl.multiple_of(j * levels, levels), levels)
            zy[t, row, :] = zy[t, row, :] + (
                v1y[t, row, :] * front_y + v2y[t, row, :] * back_y
            )
            return 0

        lax.fori_loop(0, LANES, y_finish, 0, unroll=8)

    def store(t, l):
        return pltpu.make_async_copy(
            field.at[t, pl.ds(l * cx, cx), :],
            out.at[l, :, pl.ds(t * LANES, LANES)],
            out_sem.at[t, l],
        )

    for t in range(tiles):
        for l in range(levels):
            block = jnp.transpose(zy[t, pl.ds(l, LANES, stride=levels), :])
            field[t, pl.ds(l * cx, cx), :] = block * scale_v[
                l, :, pl.ds(t * LANES, LANES)
            ].astype(jnp.float32)
            store(t, l).start()

    code_copy.wait()
    level_base = lax.broadcasted_iota(jnp.int32, (levels, LANES), 0) * points
    shift = cy.bit_length() - 1

    def ret_copy(j, turn, there, here):
        return pltpu.make_async_remote_copy(
            src_ref=send_ret.at[there],
            dst_ref=recv_ret.at[turn, here],
            send_sem=rs.at[turn, j],
            recv_sem=rr.at[turn, j],
            device_id={
                "gx": there // ny,
                "gy": lax.rem(there, ny),
                "hour": lax.rem(mh + turn, nh),
            },
            device_id_type=MESH,
        )

    def one_source(source):
        def one_slot(p, _):
            code = codes_s[source, p]
            u = jnp.minimum((code >> shift) & (cx - 1), cx - 4)
            v = code & (cy - 1)
            tile = v >> 7
            off = v & (LANES - 1)
            after = jnp.minimum(tile + 1, tiles - 1)
            row = jnp.broadcast_to(recv_obs[source, pl.ds(p, 1), :], (levels, LANES))
            ahead = (lane - off) & (LANES - 1)
            base = level_base + (ahead & 3)
            inside = lane >= off
            total = None
            for dx in range(4):
                rows = pl.ds(u + dx, levels, stride=cx)
                data = jnp.where(inside, field[tile, rows, :], field[after, rows, :])
                term = pick(row, base + 4 * dx) * data
                total = term if total is None else total + term
            acc[pl.ds(pl.multiple_of(p * levels, levels), levels), :] = jnp.where(
                ahead < 4, total, 0.0
            )
            return 0

        lax.fori_loop(0, cap, one_slot, 0, unroll=8)
        summed = acc[pl.ds(0, cap, stride=levels), :]
        for l in range(1, levels):
            summed = summed + acc[pl.ds(l, cap, stride=levels), :]
        return lax.dot_general(
            ones,
            summed,
            (((1,), (1,)), ((), ())),
            precision=EXACT,
            preferred_element_type=jnp.float32,
        )

    def each_source(j, _):
        source = lax.rem(me + j, owners)
        send_ret[source, :, :cap] = one_source(source)
        for turn in range(nh):
            ret_copy(j, turn, source, me).start()
        return 0

    lax.fori_loop(1, owners, each_source, 0)
    send_ret[me, :, :cap] = one_source(me)
    for turn in range(1, nh):
        ret_copy(0, turn, me, me).start()
    recv_ret[0, me] = send_ret[me]

    for turn in range(1, nh):
        ret_copy(0, turn, me, me).wait_recv()

    def ret_wait(j, _):
        for turn in range(nh):
            ret_copy(
                j, turn, lax.rem(me + j, owners), lax.rem(me + owners - j, owners)
            ).wait_recv()
        return 0

    lax.fori_loop(1, owners, ret_wait, 0)
    back_sum = recv_ret[0, :, 0, :cap]
    for turn in range(1, nh):
        back_sum = back_sum + recv_ret[turn, :, 0, :cap]
    spread = jnp.dot(
        back_sum, of_place[:cap], precision=EXACT, preferred_element_type=jnp.float32
    )
    modelled = jnp.sum(spread * of_owner, axis=0, keepdims=True)
    departure[...] = (modelled - innovation[...]) / sigma[...]

    for t in range(tiles):
        for l in range(levels):
            store(t, l).wait()

    def x_sent(j, _):
        x_copy(j, mx).wait_send()
        return 0

    lax.fori_loop(1, nx, x_sent, 0)
    for j in range(1, ny):
        y_copy(j, my).wait_send()

    def obs_sent(j, _):
        obs_copy(j, lax.rem(me + j, owners), me).wait_send()
        for turn in range(nh):
            ret_copy(j, turn, lax.rem(me + j, owners), me).wait_send()
        return 0

    lax.fori_loop(1, owners, obs_sent, 0)
    for turn in range(1, nh):
        ret_copy(0, turn, me, me).wait_send()


def on_device(
    dims, control, background_scale, rate_x, rate_y, obs_owner, stencil, obs_weights, innovation, obs_sigma
):
    nx, ny, nh = dims
    owners = nx * ny
    levels, cx, cy = control.shape
    tiles = cy // LANES
    obs = obs_owner.shape[0]
    cap = -(-(2 * obs // owners) // 8) * 8
    f32 = jnp.float32
    vmem = pl.BlockSpec(memory_space=pltpu.VMEM)
    hbm = pl.BlockSpec(memory_space=pl.ANY)
    dma = pltpu.SemaphoreType.DMA
    increment, departure = pl.pallas_call(
        functools.partial(kernel, (nx, ny, nh, cap)),
        out_shape=(
            jax.ShapeDtypeStruct(control.shape, f32),
            jax.ShapeDtypeStruct((1, obs), f32),
        ),
        in_specs=[hbm] * 9,
        out_specs=(hbm, vmem),
        scratch_shapes=[
            pltpu.VMEM((tiles, levels * cx, LANES), f32),
            pltpu.VMEM((levels, cx, cy), background_scale.dtype),
            pltpu.VMEM((tiles, cx * levels, LANES), f32),
            pltpu.VMEM((tiles, LANES * levels, cx), f32),
            pltpu.VMEM((cx * levels, LANES), f32),
            pltpu.VMEM((cx * levels, LANES), f32),
            pltpu.VMEM((tiles, LANES * levels, cx), f32),
            pltpu.VMEM((tiles, LANES * levels, cx), f32),
            pltpu.VMEM((nx, 2 * tiles + 2, levels, LANES), f32),
            pltpu.VMEM((ny * tiles, 4, levels, cx), f32),
            pltpu.VMEM((nx, 2 * tiles, levels, LANES), f32),
            pltpu.VMEM((ny * tiles, 2, levels, cx), f32),
            pltpu.VMEM((owners, cap + 8, LANES), f32),
            pltpu.VMEM((owners, cap + 8, LANES), f32),
            pltpu.VMEM((owners, LANES), jnp.int32),
            pltpu.SMEM((owners, LANES), jnp.int32),
            pltpu.VMEM((cap * levels, LANES), f32),
            pltpu.VMEM((owners, 8, LANES), f32),
            pltpu.VMEM((nh, owners, 8, LANES), f32),
            pltpu.VMEM(rate_x.shape, f32),
            pltpu.VMEM(rate_y.shape, f32),
            pltpu.VMEM((1, obs), jnp.int32),
            pltpu.VMEM((stencil.shape[1], obs), jnp.int32),
            pltpu.VMEM(obs_weights.shape, f32),
            pltpu.VMEM((1, obs), f32),
            pltpu.VMEM((1, obs), f32),
            dma((7,)),
            dma((tiles, levels)),
            dma((tiles, levels)),
            dma,
            dma,
            dma((nx,)),
            dma((nx,)),
            dma((ny,)),
            dma((ny,)),
            dma((owners,)),
            dma((owners,)),
            dma((nh, owners)),
            dma((nh, owners)),
        ],
        compiler_params=pltpu.CompilerParams(
            collective_id=0, has_side_effects=True, vmem_limit_bytes=56 * 1024 * 1024
        ),
    )(
        control,
        background_scale,
        rate_x,
        rate_y,
        obs_owner.reshape(1, obs),
        stencil.T,
        obs_weights,
        innovation.reshape(1, obs),
        obs_sigma.reshape(1, obs),
    )
    return increment, departure.reshape(obs)


def solution(mesh):
    dims = (mesh.shape["gx"], mesh.shape["gy"], mesh.shape["hour"])
    return jax.shard_map(
        functools.partial(on_device, dims),
        mesh=mesh,
        in_specs=(
            P(("grp", "hour"), "gx", "gy"),
            P(("grp", "hour"), "gx", "gy"),
            P(("grp", "hour"), "gx"),
            P(("grp", "hour"), None),
            P(("grp", "gx", "gy")),
            P(("grp", "gx", "gy"), None),
            P(("grp", "gx", "gy"), "hour"),
            P(("grp", "gx", "gy")),
            P(("grp", "gx", "gy")),
        ),
        out_specs=(P(("grp", "hour"), "gx", "gy"), P(("grp", "gx", "gy"))),
        check_vma=False,
    )
```

```python
import functools

import jax
import jax.numpy as jnp
from jax import lax
from jax.experimental import pallas as pl
from jax.experimental.pallas import tpu as pltpu
from jax.sharding import PartitionSpec as P

EXACT = lax.Precision.HIGHEST
MESH = pl.DeviceIdType.MESH
LANES = 128


def coefficients(rate):
    a = jnp.exp(-rate)
    series = jnp.ones_like(rate)
    small = jnp.minimum(rate, 0.5)
    for n in range(9, 1, -1):
        series = 1.0 - series * small * (1.0 / n)
    c = jnp.where(rate < 0.5, small * series, 1.0 - a)
    b = jnp.sqrt(c * (1.0 + a))
    return a, b, c


def pick(row, index):
    return jnp.take_along_axis(row, index, axis=1, mode="promise_in_bounds")


def combine(arrived, carries, count, needed, width):
    zero = tuple(jnp.zeros(carries.shape[2:], jnp.float32) for _ in range(width))

    def ahead(e, state):
        factor = arrived(e, 0, width)
        new = []
        for t in range(width):
            carries[e, t] = state[t]
            new.append(factor * state[t] + arrived(e, 0, t))
        return tuple(new)

    def behind(k, state):
        e = count - 1 - k
        factor, cross = arrived(e, 0, width), arrived(e, 1, width)
        new = []
        for t in range(width):
            carries[e, width + t] = state[t]
            new.append(
                factor * state[t] + (arrived(e, 1, t) + cross * carries[e, t])
            )
        return tuple(new)

    lax.fori_loop(0, count, ahead, zero)
    lax.fori_loop(0, needed, behind, zero)


def kernel(
    dims,
    control,
    scale,
    rate_x_h,
    rate_y_h,
    owner_h,
    stencil_h,
    weights_h,
    innovation_h,
    sigma_h,
    out,
    departure,
    field,
    scale_v,
    zx,
    zy,
    v1x,
    v2x,
    v1y,
    v2y,
    ay,
    by,
    cyg,
    edges_x,
    edges_y,
    carry_x,
    carry_y,
    send_obs,
    recv_obs,
    codes_v,
    codes_s,
    acc,
    sums,
    send_ret,
    recv_ret,
    rate_x,
    rate_y,
    owner,
    stencil,
    weights,
    innovation,
    sigma,
    small_sem,
    in_sem,
    out_sem,
    scale_sem,
    code_sem,
    xs,
    xr,
    ys,
    yr,
    os_,
    or_,
    rs,
    rr,
):
    nx, ny, nh, cap = dims
    owners = nx * ny
    levels, cx, cy = control.shape
    tiles = cy // LANES
    obs = owner.shape[1]
    mx, my, mh = lax.axis_index("gx"), lax.axis_index("gy"), lax.axis_index("hour")
    me = mx * ny + my
    world = owners * nh
    rank = me * nh + mh

    barrier = pltpu.get_barrier_semaphore()

    def greet(j, _):
        other = lax.rem(rank + j, world)
        pl.semaphore_signal(
            barrier,
            inc=1,
            device_id={
                "gx": other // (ny * nh),
                "gy": lax.rem(other // nh, ny),
                "hour": lax.rem(other, nh),
            },
            device_id_type=MESH,
        )
        return 0

    def load(t, l):
        return pltpu.make_async_copy(
            control.at[l, :, pl.ds(t * LANES, LANES)],
            field.at[t, pl.ds(l * cx, cx), :],
            in_sem.at[t, l],
        )

    small = [
        pltpu.make_async_copy(source, place, small_sem.at[n])
        for n, (source, place) in enumerate(
            (
                (rate_x_h, rate_x),
                (owner_h, owner),
                (stencil_h, stencil),
                (weights_h, weights),
                (rate_y_h, rate_y),
                (innovation_h, innovation),
                (sigma_h, sigma),
            )
        )
    ]
    small[0].start()
    for t in range(tiles):
        for l in range(levels):
            load(t, l).start()
    for copy in small[1:]:
        copy.start()
    scale_copy = pltpu.make_async_copy(scale, scale_v, scale_sem)
    scale_copy.start()
    lax.fori_loop(1, world, greet, 0)

    lane = lax.broadcasted_iota(jnp.int32, (levels, LANES), 1)
    ones = jnp.ones((levels, LANES), jnp.float32)
    zeros = jnp.zeros((levels, LANES), jnp.float32)

    small[0].wait()
    ax, bx, cxg = coefficients(rate_x[...])
    for t in range(tiles):
        for l in range(levels):
            load(t, l).wait()

    def x_forward(i, state):
        at = lane * 0 + i
        a, b = pick(ax, at), pick(bx, at)
        row = pl.ds(pl.multiple_of(i * levels, levels), levels)
        new = []
        for t in range(tiles):
            s = a * state[t] + b * field[t, pl.ds(i, levels, stride=cx), :]
            zx[t, row, :] = s
            new.append(s)
        lead = a * state[tiles]
        v1x[row, :] = lead
        return tuple(new) + (lead,)

    state = lax.fori_loop(0, cx, x_forward, (zeros,) * tiles + (ones,), unroll=8)
    for t in range(tiles):
        edges_x[mx, 0, t] = state[t]
    edges_x[mx, 0, tiles] = state[tiles]
    pl.semaphore_wait(barrier, world - 1)

    def x_copy(half, j, place, there):
        return pltpu.make_async_remote_copy(
            src_ref=edges_x.at[place, half],
            dst_ref=edges_x.at[place, half],
            send_sem=xs.at[half, j],
            recv_sem=xr.at[half, j],
            device_id={"gx": there},
            device_id_type=MESH,
        )

    def x_start(j, _):
        x_copy(0, j, mx, lax.rem(mx + j, nx)).start()
        return 0

    lax.fori_loop(1, nx, x_start, 0)

    def x_backward(k, state):
        i = cx - 1 - k
        at = lane * 0 + i
        a, c = pick(ax, at), pick(cxg, at)
        row = pl.ds(pl.multiple_of(i * levels, levels), levels)
        new = []
        for t in range(tiles):
            s = a * state[t] + c * zx[t, row, :]
            zx[t, row, :] = s
            new.append(s)
        cross = a * state[tiles] + c * v1x[row, :]
        v1x[row, :] = cross
        trail = a * state[tiles + 1]
        v2x[row, :] = trail
        return tuple(new) + (cross, trail)

    state = lax.fori_loop(0, cx, x_backward, (zeros,) * (tiles + 1) + (ones,), unroll=8)
    for t in range(tiles):
        edges_x[mx, 1, t] = state[t]
    edges_x[mx, 1, tiles] = state[tiles]

    def x_start_back(j, _):
        x_copy(1, j, mx, mx - j).start()
        return 0

    lax.fori_loop(1, mx + 1, x_start_back, 0)

    for copy in small[1:]:
        copy.wait()
    own = owner[...]
    own_col = jnp.transpose(jnp.broadcast_to(own.astype(jnp.float32), (8, obs)))[:, :1]
    earlier = lax.broadcasted_iota(jnp.int32, (obs, obs), 0) < lax.broadcasted_iota(
        jnp.int32, (obs, obs), 1
    )
    same = earlier & (own_col == own.astype(jnp.float32))
    place = jnp.sum(jnp.where(same, 1.0, 0.0), axis=0, keepdims=True).astype(jnp.int32)
    cells = stencil[...]
    points = cells.shape[0]
    corner = jnp.min(cells, axis=0, keepdims=True)
    j_row = lax.broadcasted_iota(jnp.int32, (points, obs), 0)
    wanted = corner + (j_row // 4) * cy + lax.rem(j_row, 4)
    order = jnp.zeros((points, obs), jnp.int32)
    for s in range(1, points):
        order = jnp.where(cells[s : s + 1, :] == wanted, s, order)
    order = jnp.concatenate([order + points * l for l in range(levels)], axis=0)
    order = jnp.transpose(order.astype(jnp.float32)).astype(jnp.int32)
    sorted_weights = pick(weights[...], order)
    target = own * cap + place
    slots = owners * cap
    chosen = jnp.where(
        lax.broadcasted_iota(jnp.int32, (slots, obs), 0) == target, 1.0, 0.0
    )
    packed = jnp.dot(
        chosen, sorted_weights, precision=EXACT, preferred_element_type=jnp.float32
    )
    send_obs[:, :cap, :] = packed.reshape(owners, cap, LANES)
    of_owner = jnp.where(
        lax.broadcasted_iota(jnp.int32, (owners, obs), 0) == own, 1.0, 0.0
    )
    of_place = jnp.where(
        lax.broadcasted_iota(jnp.int32, (LANES, obs), 0) == place, 1.0, 0.0
    )
    codes = lax.dot_general(
        of_owner * corner.astype(jnp.float32),
        of_place,
        (((1,), (1,)), ((), ())),
        precision=EXACT,
        preferred_element_type=jnp.float32,
    )
    send_obs[:, cap:, :] = jnp.broadcast_to(codes[:, None, :], (owners, 8, LANES))
    recv_obs[me] = send_obs[me]

    def obs_copy(j, there, here):
        return pltpu.make_async_remote_copy(
            src_ref=send_obs.at[there],
            dst_ref=recv_obs.at[here],
            send_sem=os_.at[j],
            recv_sem=or_.at[j],
            device_id={"gx": there // ny, "gy": lax.rem(there, ny)},
            device_id_type=MESH,
        )

    def obs_start(j, _):
        obs_copy(j, lax.rem(me + j, owners), me).start()
        return 0

    lax.fori_loop(1, owners, obs_start, 0)

    for t in range(tiles):
        gains = coefficients(
            rate_y[:, pl.ds(pl.multiple_of(my * cy + t * LANES, LANES), LANES)]
        )

        def y_lead(j, lead, t=t, gains=gains):
            at = lane * 0 + j
            row = pl.ds(pl.multiple_of(j * levels, levels), levels)
            a = pick(gains[0], at)
            ay[t, row, :] = a
            by[t, row, :] = pick(gains[1], at)
            lead = a * lead
            v1y[t, row, :] = lead
            return lead

        edges_y[my, 0, tiles + t] = lax.fori_loop(0, LANES, y_lead, ones, unroll=8)

        def y_cross(k, state, t=t, gains=gains):
            j = LANES - 1 - k
            at = lane * 0 + j
            row = pl.ds(pl.multiple_of(j * levels, levels), levels)
            a, c = ay[t, row, :], pick(gains[2], at)
            cyg[t, row, :] = c
            cross = a * state[0] + c * v1y[t, row, :]
            v1y[t, row, :] = cross
            trail = a * state[1]
            v2y[t, row, :] = trail
            return cross, trail

        edges_y[my, 1, tiles + t] = lax.fori_loop(
            0, LANES, y_cross, (zeros, ones), unroll=8
        )[0]

    def x_wait(j, _):
        x_copy(0, j, lax.rem(mx + nx - j, nx), lax.rem(mx + j, nx)).wait_recv()
        return 0

    lax.fori_loop(1, nx, x_wait, 0)

    def x_wait_back(j, _):
        x_copy(1, j, mx + j, lax.rem(mx + j, nx)).wait_recv()
        return 0

    lax.fori_loop(1, nx - mx, x_wait_back, 0)
    combine(lambda e, half, t: edges_x[e, half, t], carry_x, nx, nx - mx, tiles)
    front = [carry_x[mx, t] for t in range(tiles)]
    back = [carry_x[mx, tiles + t] for t in range(tiles)]

    def x_finish(i, _):
        row = pl.ds(pl.multiple_of(i * levels, levels), levels)
        lead, trail = v1x[row, :], v2x[row, :]
        for t in range(tiles):
            zx[t, row, :] = zx[t, row, :] + (lead * front[t] + trail * back[t])
        return 0

    lax.fori_loop(0, cx, x_finish, 0, unroll=8)

    for t in range(tiles):
        for l in range(levels):
            zy[t, pl.ds(l, LANES, stride=levels), :] = jnp.transpose(
                zx[t, pl.ds(l, cx, stride=levels), :]
            )

    def y_forward(j, state):
        row = pl.ds(pl.multiple_of(j * levels, levels), levels)
        new = []
        for t in range(tiles):
            value = ay[t, row, :] * state[t] + by[t, row, :] * zy[t, row, :]
            zy[t, row, :] = value
            new.append(value)
        return tuple(new)

    state = lax.fori_loop(0, LANES, y_forward, (zeros,) * tiles, unroll=8)
    for t in range(tiles):
        edges_y[my, 0, t] = state[t]

    def y_copy(half, j, place, there):
        return pltpu.make_async_remote_copy(
            src_ref=edges_y.at[place, half],
            dst_ref=edges_y.at[place, half],
            send_sem=ys.at[half, j],
            recv_sem=yr.at[half, j],
            device_id={"gy": there},
            device_id_type=MESH,
        )

    for j in range(1, ny):
        y_copy(0, j, my, lax.rem(my + j, ny)).start()

    def y_backward(k, state):
        j = LANES - 1 - k
        row = pl.ds(pl.multiple_of(j * levels, levels), levels)
        new = []
        for t in range(tiles):
            value = ay[t, row, :] * state[t] + cyg[t, row, :] * zy[t, row, :]
            zy[t, row, :] = value
            new.append(value)
        return tuple(new)

    state = lax.fori_loop(0, LANES, y_backward, (zeros,) * tiles, unroll=8)
    for t in range(tiles):
        edges_y[my, 1, t] = state[t]

    def y_start_back(j, _):
        y_copy(1, j, my, my - j).start()
        return 0

    lax.fori_loop(1, my + 1, y_start_back, 0)

    def obs_wait(j, _):
        obs_copy(j, lax.rem(me + j, owners), lax.rem(me + owners - j, owners)).wait_recv()
        return 0

    lax.fori_loop(1, owners, obs_wait, 0)
    codes_v[...] = recv_obs[:, cap, :].astype(jnp.int32)
    code_copy = pltpu.make_async_copy(codes_v, codes_s, code_sem)
    code_copy.start()
    scale_copy.wait()

    for j in range(1, ny):
        y_copy(0, j, lax.rem(my + ny - j, ny), lax.rem(my + j, ny)).wait_recv()

    def y_wait_back(j, _):
        y_copy(1, j, my + j, lax.rem(my + j, ny)).wait_recv()
        return 0

    lax.fori_loop(1, ny - my, y_wait_back, 0)
    combine(
        lambda e, half, t: edges_y[e // tiles, half, t * tiles + lax.rem(e, tiles)],
        carry_y,
        ny * tiles,
        (ny - my) * tiles,
        1,
    )

    for t in range(tiles):
        front_y = carry_y[my * tiles + t, 0]
        back_y = carry_y[my * tiles + t, 1]

        def y_finish(j, _, t=t, front_y=front_y, back_y=back_y):
            row = pl.ds(pl.multiple_of(j * levels, levels), levels)
            zy[t, row, :] = zy[t, row, :] + (
                v1y[t, row, :] * front_y + v2y[t, row, :] * back_y
            )
            return 0

        lax.fori_loop(0, LANES, y_finish, 0, unroll=8)

    def store(t, l):
        return pltpu.make_async_copy(
            field.at[t, pl.ds(l * cx, cx), :],
            out.at[l, :, pl.ds(t * LANES, LANES)],
            out_sem.at[t, l],
        )

    for t in range(tiles):
        for l in range(levels):
            block = jnp.transpose(zy[t, pl.ds(l, LANES, stride=levels), :])
            block = block * scale_v[l, :, pl.ds(t * LANES, LANES)].astype(jnp.float32)
            field[t, pl.ds(l * cx, cx), :] = block
            zx[t, pl.ds(l, cx, stride=levels), :] = block
            store(t, l).start()

    code_copy.wait()
    level_base = lax.broadcasted_iota(jnp.int32, (levels, LANES), 0) * points
    shift = cy.bit_length() - 1

    def ret_copy(j, turn, there, here):
        return pltpu.make_async_remote_copy(
            src_ref=send_ret.at[there * cap // LANES],
            dst_ref=recv_ret.at[turn, here],
            send_sem=rs.at[turn, j],
            recv_sem=rr.at[turn, j],
            device_id={
                "gx": there // ny,
                "gy": lax.rem(there, ny),
                "hour": lax.rem(mh + turn, nh),
            },
            device_id_type=MESH,
        )

    def one_source(source):
        def one_slot(p, _):
            code = codes_s[source, p]
            u = jnp.minimum((code >> shift) & (cx - 1), cx - 4)
            v = code & (cy - 1)
            tile = v >> 7
            off = v & (LANES - 1)
            after = jnp.minimum(tile + 1, tiles - 1)
            row = jnp.broadcast_to(recv_obs[source, pl.ds(p, 1), :], (levels, LANES))
            ahead = (lane - off) & (LANES - 1)
            base = level_base + (ahead & 3)
            inside = lane >= off
            total = None
            for dx in range(4):
                rows = pl.ds((u + dx) * levels, levels)
                data = jnp.where(inside, zx[tile, rows, :], zx[after, rows, :])
                term = pick(row, base + 4 * dx) * data
                total = term if total is None else total + term
            acc[pl.ds(pl.multiple_of(p * levels, levels), levels), :] = jnp.where(
                ahead < 4, total, 0.0
            )
            return 0

        lax.fori_loop(0, cap, one_slot, 0, unroll=8)
        summed = acc[pl.ds(0, cap, stride=levels), :]
        for l in range(1, levels):
            summed = summed + acc[pl.ds(l, cap, stride=levels), :]
        sums[pl.ds(pl.multiple_of(source * cap, 8), cap), :] = summed

    def each_source(source, _):
        one_source(source)
        return 0

    lax.fori_loop(0, owners, each_source, 0)
    for n in range(slots // LANES):
        send_ret[n] = lax.dot_general(
            ones,
            sums[n * LANES : (n + 1) * LANES, :],
            (((1,), (1,)), ((), ())),
            precision=EXACT,
            preferred_element_type=jnp.float32,
        )

    def ret_start(j, _):
        for turn in range(nh):
            ret_copy(j, turn, lax.rem(me + j, owners), me).start()
        return 0

    lax.fori_loop(1, owners, ret_start, 0)
    for turn in range(1, nh):
        ret_copy(0, turn, me, me).start()
    recv_ret[0, me] = send_ret[me * cap // LANES]

    for turn in range(1, nh):
        ret_copy(0, turn, me, me).wait_recv()

    def ret_wait(j, _):
        for turn in range(nh):
            ret_copy(
                j, turn, lax.rem(me + j, owners), lax.rem(me + owners - j, owners)
            ).wait_recv()
        return 0

    lax.fori_loop(1, owners, ret_wait, 0)
    back_sum = recv_ret[0, :, 0, :]
    for turn in range(1, nh):
        back_sum = back_sum + recv_ret[turn, :, 0, :]
    of_lane = jnp.where(
        lax.broadcasted_iota(jnp.int32, (LANES, obs), 0)
        == place + lax.rem(me * cap, LANES),
        1.0,
        0.0,
    )
    spread = jnp.dot(
        back_sum, of_lane, precision=EXACT, preferred_element_type=jnp.float32
    )
    modelled = jnp.sum(spread * of_owner, axis=0, keepdims=True)
    departure[...] = (modelled - innovation[...]) / sigma[...]

    for t in range(tiles):
        for l in range(levels):
            store(t, l).wait()

    def x_sent(j, _):
        x_copy(0, j, mx, lax.rem(mx + j, nx)).wait_send()
        return 0

    lax.fori_loop(1, nx, x_sent, 0)

    def x_sent_back(j, _):
        x_copy(1, j, mx, mx - j).wait_send()
        return 0

    lax.fori_loop(1, mx + 1, x_sent_back, 0)
    for j in range(1, ny):
        y_copy(0, j, my, lax.rem(my + j, ny)).wait_send()

    def y_sent_back(j, _):
        y_copy(1, j, my, my - j).wait_send()
        return 0

    lax.fori_loop(1, my + 1, y_sent_back, 0)

    def obs_sent(j, _):
        obs_copy(j, lax.rem(me + j, owners), me).wait_send()
        for turn in range(nh):
            ret_copy(j, turn, lax.rem(me + j, owners), me).wait_send()
        return 0

    lax.fori_loop(1, owners, obs_sent, 0)
    for turn in range(1, nh):
        ret_copy(0, turn, me, me).wait_send()


def on_device(
    dims, control, background_scale, rate_x, rate_y, obs_owner, stencil, obs_weights, innovation, obs_sigma
):
    nx, ny, nh = dims
    owners = nx * ny
    levels, cx, cy = control.shape
    tiles = cy // LANES
    obs = obs_owner.shape[0]
    cap = -(-(2 * obs // owners) // 8) * 8
    f32 = jnp.float32
    vmem = pl.BlockSpec(memory_space=pltpu.VMEM)
    hbm = pl.BlockSpec(memory_space=pltpu.HBM)
    dma = pltpu.SemaphoreType.DMA
    increment, departure = pl.pallas_call(
        functools.partial(kernel, (nx, ny, nh, cap)),
        out_shape=(
            jax.ShapeDtypeStruct(control.shape, f32),
            jax.ShapeDtypeStruct((1, obs), f32),
        ),
        in_specs=[hbm] * 9,
        out_specs=(pl.BlockSpec(memory_space=pl.ANY), vmem),
        scratch_shapes=[
            pltpu.VMEM((tiles, levels * cx, LANES), f32),
            pltpu.VMEM((levels, cx, cy), background_scale.dtype),
            pltpu.VMEM((tiles, cx * levels, LANES), f32),
            pltpu.VMEM((tiles, LANES * levels, cx), f32),
            pltpu.VMEM((cx * levels, LANES), f32),
            pltpu.VMEM((cx * levels, LANES), f32),
            pltpu.VMEM((tiles, LANES * levels, cx), f32),
            pltpu.VMEM((tiles, LANES * levels, cx), f32),
            pltpu.VMEM((tiles, LANES * levels, LANES), f32),
            pltpu.VMEM((tiles, LANES * levels, LANES), f32),
            pltpu.VMEM((tiles, LANES * levels, LANES), f32),
            pltpu.VMEM((nx, 2, tiles + 1, levels, LANES), f32),
            pltpu.VMEM((ny, 2, 2 * tiles, levels, cx), f32),
            pltpu.VMEM((nx, 2 * tiles, levels, LANES), f32),
            pltpu.VMEM((ny * tiles, 2, levels, cx), f32),
            pltpu.VMEM((owners, cap + 8, LANES), f32),
            pltpu.VMEM((owners, cap + 8, LANES), f32),
            pltpu.VMEM((owners, LANES), jnp.int32),
            pltpu.SMEM((owners, LANES), jnp.int32),
            pltpu.VMEM((cap * levels, LANES), f32),
            pltpu.VMEM((owners * cap, LANES), f32),
            pltpu.VMEM((owners * cap // LANES, 8, LANES), f32),
            pltpu.VMEM((nh, owners, 8, LANES), f32),
            pltpu.VMEM(rate_x.shape, f32),
            pltpu.VMEM(rate_y.shape, f32),
            pltpu.VMEM((1, obs), jnp.int32),
            pltpu.VMEM((stencil.shape[1], obs), jnp.int32),
            pltpu.VMEM(obs_weights.shape, f32),
            pltpu.VMEM((1, obs), f32),
            pltpu.VMEM((1, obs), f32),
            dma((7,)),
            dma((tiles, levels)),
            dma((tiles, levels)),
            dma,
            dma,
            dma((2, nx)),
            dma((2, nx)),
            dma((2, ny)),
            dma((2, ny)),
            dma((owners,)),
            dma((owners,)),
            dma((nh, owners)),
            dma((nh, owners)),
        ],
        compiler_params=pltpu.CompilerParams(
            collective_id=0, has_side_effects=True, vmem_limit_bytes=56 * 1024 * 1024
        ),
    )(
        control,
        background_scale,
        rate_x,
        rate_y,
        obs_owner.reshape(1, obs),
        stencil.T,
        obs_weights,
        innovation.reshape(1, obs),
        obs_sigma.reshape(1, obs),
    )
    return increment, departure.reshape(obs)


def solution(mesh):
    dims = (mesh.shape["gx"], mesh.shape["gy"], mesh.shape["hour"])
    return jax.shard_map(
        functools.partial(on_device, dims),
        mesh=mesh,
        in_specs=(
            P(("grp", "hour"), "gx", "gy"),
            P(("grp", "hour"), "gx", "gy"),
            P(("grp", "hour"), "gx"),
            P(("grp", "hour"), None),
            P(("grp", "gx", "gy")),
            P(("grp", "gx", "gy"), None),
            P(("grp", "gx", "gy"), "hour"),
            P(("grp", "gx", "gy")),
            P(("grp", "gx", "gy")),
        ),
        out_specs=(P(("grp", "hour"), "gx", "gy"), P(("grp", "gx", "gy"))),
        check_vma=False,
    )
```
